32 devices in a mesh: dp: 8 (over z, y), own: 4 (over x, core).
Axes of the slice: x: 2, y: 2, z: 4, core: 2. Of those that a mesh axis runs over, the one named last changes fastest.
Arguments:
- tokens: bfloat16 [8192, 2560], P('dp'), may hold values from -6 to 6
- route_w: float32 [8192, 2], P('dp'), may hold values from 0.1 to 1
- w_gate: bfloat16 [4, 2560, 768], P('own', 'dp'), may hold values from -0.125 to 0.125
- w_up: bfloat16 [4, 2560, 768], P('own', 'dp'), may hold values from -0.125 to 0.125
- slot_token: int32 [8, 4, 512], P('dp', 'own'), may hold values from 0 to 1023, as said below
- slot_pick: int32 [8, 4, 512], P('dp', 'own'), may hold values from 0 to 1
- live_blocks: int32 [8, 4], P('dp', 'own'), may hold values from 1 to 4, as said below
- d_hidden: bfloat16 [8, 4, 512, 768], P('dp', 'own'), may hold values from -6 to 6
Outputs:
- hidden: bfloat16 [8, 4, 512, 768], P('dp', 'own')
- grad_gate: float32 [4, 2560, 768], P('own', 'dp')
- grad_up: float32 [4, 2560, 768], P('own', 'dp')
- d_tokens: bfloat16 [8192, 2560], P(('dp', 'own'))
- d_route: float32 [8192, 2], P(('dp', 'own'))
The draws below stay inside these ranges and needn't reach their ends.
Inputs may be any that keep to these rules, and one draw needn't show every extreme that they name: For each index of dp the pairs (slot_token, slot_pick) over all experts and all 512 slots are distinct. `live_blocks`: 4 is reached by some entry.
All inputs are finite; a program needn't handle non-finite values.
Results may differ from the reference program's by a relative error of at most 0.0052.
Values may be sent and summed in bfloat16 or wider, within the bound.
A program may use at most 128 MiB of HBM per device.

```python
import math
import jax
import jax.numpy as jnp
from jax import lax

D = 2560
HW = 768
TOPK = 2
BLK = 128
TOK_DEV = 1024
EXPERTS = 4
NBLK = 4
TOKENS = 8192
N_DP = 8


def routing_tables(key):
    key_list = jax.random.split(jax.random.fold_in(key, 11), N_DP)

    def permute_one(single_key):
        return jax.random.permutation(single_key, TOK_DEV * TOPK)
    permuted = jax.vmap(permute_one)(key_list)
    pair_ids = permuted[:, :EXPERTS * NBLK * BLK].reshape(N_DP, EXPERTS, NBLK * BLK)
    return ((pair_ids // TOPK).astype(jnp.int32), (pair_ids % TOPK).astype(jnp.int32))


def draw_slot_token(key, part):
    return routing_tables(key)[0]


def draw_slot_pick(key, part):
    return routing_tables(key)[1]


def draw_live_blocks(key, part):
    factor_one = jax.random.randint(jax.random.fold_in(key, 31), (N_DP, EXPERTS), 0, NBLK, dtype=jnp.int32)
    factor_two = jax.random.randint(jax.random.fold_in(key, 37), (N_DP, EXPERTS), 0, NBLK, dtype=jnp.int32)
    counts = 1 + factor_one * factor_two // max(NBLK - 1, 1)
    chosen_row = jax.random.randint(jax.random.fold_in(key, 41), (), 0, N_DP, dtype=jnp.int32)
    chosen_col = jax.random.randint(jax.random.fold_in(key, 43), (), 0, EXPERTS, dtype=jnp.int32)
    rows_grid = lax.broadcasted_iota(jnp.int32, (N_DP, EXPERTS), 0)
    cols_grid = lax.broadcasted_iota(jnp.int32, (N_DP, EXPERTS), 1)
    chosen = (rows_grid == chosen_row) & (cols_grid == chosen_col)
    return jnp.where(chosen, NBLK, counts).astype(jnp.int32)


def spiked(values, stream_key, source, target, parts, factor):
    def block_of(position):
        return (jnp.arange(values.shape[position]) // (values.shape[position] // parts)).reshape((-1,) + (1,) * (values.ndim - 1 - position))

    first = jax.random.permutation(stream_key, parts)[block_of(target)]
    far = (block_of(target) + parts // 2) % parts
    return jnp.where((block_of(source) == first) | (block_of(source) == far), factor * values, values)


def steps_of(rng, dims, pieces, smallest, high):
    factor_of = 1.0
    for dim, shards_of in pieces:
        steps = jax.random.uniform(jax.random.fold_in(jax.random.fold_in(rng, 6), dim), (shards_of,), jnp.float32, smallest / len(pieces), high / len(pieces))
        factor_of = factor_of * jnp.repeat(jnp.exp(steps), dims[dim] // shards_of).reshape((-1,) + (1,) * (len(dims) - 1 - dim))
    return factor_of


def gaussian(key, dims, deviation, reach, cuts=(), kind=jnp.bfloat16):
    array = jax.random.normal(key, dims, jnp.float32) * deviation
    if len(cuts) > 0:
        array = steps_of(key, dims, cuts, -0.22, 0.18) * array
    return jnp.clip(array, min=-reach, max=reach).astype(kind)


def noise_with(rng, dims, scale, bound, shards, heavy, kind=jnp.bfloat16):
    values = scale * jax.random.normal(rng, dims, jnp.float32)
    if shards:
        values = values * steps_of(rng, dims, shards, -0.22, 0.18)
    return jnp.clip(spiked(values, jax.random.fold_in(rng, 3), *heavy), -bound, bound).astype(kind)


def setup_inputs(seed: int = 0) -> dict:
    arg_keys = jax.random.split(jax.random.key(seed), 9)
    return {
        "tokens": noise_with(arg_keys[0], (TOKENS, D), 1.0, 6.0, ((0, 8),), (0, 1, 8, 2.0)),
        "route_w": jnp.clip(jnp.exp(math.log(1.0) - 2.3025851 * jax.random.uniform(arg_keys[1], (TOKENS, TOPK), jnp.float32) ** steps_of(arg_keys[1], (TOKENS, TOPK), ((0, 8),), -0.2, 0.2)), 0.1, 1.0),
        "w_gate": gaussian(arg_keys[2], (EXPERTS, D, HW), D ** -0.5, 0.125, ((0, 4), (1, 8))),
        "w_up": gaussian(arg_keys[3], (EXPERTS, D, HW), D ** -0.5, 0.125, ((0, 4), (1, 8))),
        "slot_token": draw_slot_token(jax.random.fold_in(arg_keys[8], 71), 0),
        "slot_pick": draw_slot_pick(jax.random.fold_in(arg_keys[8], 71), 0),
        "live_blocks": draw_live_blocks(jax.random.fold_in(arg_keys[8], 71), 0),
        "d_hidden": gaussian(arg_keys[7], (N_DP, EXPERTS, NBLK * BLK, HW), 1.0, 6.0, ((0, 8), (1, 4))),
    }


def finish(pre_gate, pre_up, block_gate, block_cot):
    sigmoid_gate = jax.nn.sigmoid(pre_gate)
    activated = pre_gate * sigmoid_gate
    block_hidden = (activated * pre_up * block_gate).astype(jnp.bfloat16)
    scaled_cot = block_cot * block_gate
    grad_pre = scaled_cot * pre_up * sigmoid_gate * (1.0 + pre_gate * (1.0 - sigmoid_gate))
    grad_up_pre = scaled_cot * activated
    grad_cat = jnp.concatenate((grad_pre.astype(jnp.bfloat16), grad_up_pre.astype(jnp.bfloat16)), axis=1)
    route_grad = lax.optimization_barrier(jnp.sum(block_cot * activated * pre_up, axis=1))
    return (block_hidden, grad_cat, route_grad)

def run_blocks(rows_x, gate_col, cot_all, w_full, live_count):
    capacity = rows_x.shape[0]
    hidden_width = w_full.shape[1] // 2
    initial = (jnp.zeros((capacity, hidden_width), jnp.bfloat16), jnp.zeros((capacity, 2 * hidden_width), jnp.bfloat16), jnp.zeros((capacity, w_full.shape[0]), jnp.float32), jnp.zeros((capacity,), jnp.float32))

    def block_step(block_index, state_now):
        hidden, grad_cat, token_grad_rows, route_grad = state_now
        first = (block_index * BLK).astype(jnp.int32)
        block_rows = lax.dynamic_slice_in_dim(rows_x, first, BLK, 0)
        block_gate = lax.dynamic_slice_in_dim(gate_col, first, BLK, 0)[:, None]
        block_cot = lax.dynamic_slice_in_dim(cot_all, first, BLK, 0).astype(jnp.float32)
        projected = jnp.dot(block_rows, w_full, preferred_element_type=jnp.float32)
        block_hidden, block_dcat, block_route = finish(projected[:, :hidden_width], projected[:, hidden_width:], block_gate, block_cot)
        block_tgrad = lax.dot_general(block_dcat, w_full, (((1,), (1,)), ((), ())), preferred_element_type=jnp.float32)
        hidden = lax.dynamic_update_slice_in_dim(hidden, block_hidden, first, 0)
        grad_cat = lax.dynamic_update_slice_in_dim(grad_cat, block_dcat, first, 0)
        token_grad_rows = lax.dynamic_update_slice_in_dim(token_grad_rows, block_tgrad, first, 0)
        route_grad = lax.dynamic_update_slice_in_dim(route_grad, block_route, first, 0)
        return (hidden, grad_cat, token_grad_rows, route_grad)
    return lax.fori_loop(jnp.int32(0), jnp.asarray(live_count).astype(jnp.int32), block_step, initial)

def weight_sum(rows_x, grad_cat, live_count, offset, length):
    offset_index = jnp.asarray(offset).astype(jnp.int32)

    def add_block(block_index, running):
        first = (block_index * BLK).astype(jnp.int32)
        block_rows = lax.dynamic_slice(rows_x, (first, offset_index), (BLK, length))
        block_dcat = lax.dynamic_slice_in_dim(grad_cat, first, BLK, 0)
        return running + lax.dot_general(block_rows, block_dcat, (((0,), (0,)), ((), ())), preferred_element_type=jnp.float32)
    return lax.fori_loop(jnp.int32(0), jnp.asarray(live_count).astype(jnp.int32), add_block, jnp.zeros((length, grad_cat.shape[1]), jnp.float32))

def reference(tokens, route_w, w_gate, w_up, slot_token, slot_pick, live_blocks, d_hidden):
    w_cat = jnp.concatenate((w_gate, w_up), axis=2)
    grad_scale = 1.0 / math.sqrt(TOKENS)

    def per_shard(grad_total, shard_index):
        start_row = (shard_index * TOK_DEV).astype(jnp.int32)
        local_tokens = lax.dynamic_slice_in_dim(tokens, start_row, TOK_DEV, 0)
        gate_table = lax.dynamic_slice_in_dim(route_w, start_row, TOK_DEV, 0)
        token_sum = jnp.zeros((TOK_DEV, D), jnp.float32)
        route_sum = jnp.zeros((TOK_DEV, TOPK), jnp.float32)
        hiddens = []
        for expert in range(EXPERTS):
            tok_all = slot_token[shard_index, expert]
            pick_all = slot_pick[shard_index, expert]
            live_count = live_blocks[shard_index, expert]
            rows_x = local_tokens[tok_all]
            gate_col = gate_table[tok_all, pick_all]
            hidden, grad_cat, token_grad_rows, route_grad = run_blocks(rows_x, gate_col, d_hidden[shard_index, expert], w_cat[expert], live_count)
            token_grad = jnp.zeros((TOK_DEV, D), jnp.float32).at[tok_all].add(token_grad_rows)
            route_part = jnp.zeros((TOK_DEV, TOPK), jnp.float32).at[tok_all, pick_all].add(route_grad)
            token_sum = token_sum + lax.optimization_barrier(token_grad.astype(jnp.bfloat16)).astype(jnp.float32)
            route_sum = route_sum + lax.optimization_barrier(route_part.astype(jnp.bfloat16)).astype(jnp.float32)
            grad_total = grad_total.at[expert].add(weight_sum(rows_x, grad_cat, live_count, 0, D))
            hiddens.append(hidden)
        return (grad_total, (jnp.stack(hiddens), token_sum.astype(jnp.bfloat16), route_sum))
    initial = jnp.zeros((EXPERTS, D, 2 * HW), jnp.float32)
    grad_total, outputs = lax.scan(per_shard, initial, jnp.arange(N_DP, dtype=jnp.int32))
    hidden, d_tokens, d_route = outputs
    grad_total = grad_total * grad_scale
    return (hidden, grad_total[:, :, :HW], grad_total[:, :, HW:], d_tokens.reshape(TOKENS, D), d_route.reshape(TOKENS, TOPK))
```

```python
import math
import functools

import jax
import jax.numpy as jnp
from jax import lax
from jax.experimental import pallas as pl
from jax.experimental.pallas import tpu as pltpu
from jax.sharding import PartitionSpec as P

BLK = 128
F32 = jnp.float32
BF16 = jnp.bfloat16


def finish(pre_gate, pre_up, block_gate, block_cot):
    sigmoid_gate = jax.nn.sigmoid(pre_gate)
    activated = pre_gate * sigmoid_gate
    block_hidden = (activated * pre_up * block_gate).astype(jnp.bfloat16)
    scaled_cot = block_cot * block_gate
    grad_pre = scaled_cot * pre_up * sigmoid_gate * (1.0 + pre_gate * (1.0 - sigmoid_gate))
    grad_up_pre = scaled_cot * activated
    grad_cat = jnp.concatenate(
        (grad_pre.astype(jnp.bfloat16), grad_up_pre.astype(jnp.bfloat16)), axis=1
    )
    route_grad = jnp.sum(block_cot * activated * pre_up, axis=1)
    return (block_hidden, grad_cat, route_grad)


def run_blocks(rows_x, gate_col, cot_all, w_full, live_count):
    capacity = rows_x.shape[0]
    hidden_width = w_full.shape[1] // 2
    initial = (
        jnp.zeros((capacity, hidden_width), jnp.bfloat16),
        jnp.zeros((capacity, 2 * hidden_width), jnp.bfloat16),
        jnp.zeros((capacity, w_full.shape[0]), jnp.float32),
        jnp.zeros((capacity,), jnp.float32),
    )

    def block_step(block_index, state_now):
        hidden, grad_cat, token_grad_rows, route_grad = state_now
        first = (block_index * BLK).astype(jnp.int32)
        block_rows = lax.dynamic_slice_in_dim(rows_x, first, BLK, 0)
        block_gate = lax.dynamic_slice_in_dim(gate_col, first, BLK, 0)[:, None]
        block_cot = lax.dynamic_slice_in_dim(cot_all, first, BLK, 0).astype(jnp.float32)
        projected = jnp.dot(block_rows, w_full, preferred_element_type=jnp.float32)
        block_hidden, block_dcat, block_route = finish(
            projected[:, :hidden_width], projected[:, hidden_width:], block_gate, block_cot
        )
        block_tgrad = lax.dot_general(
            block_dcat, w_full, (((1,), (1,)), ((), ())), preferred_element_type=jnp.float32
        )
        hidden = lax.dynamic_update_slice_in_dim(hidden, block_hidden, first, 0)
        grad_cat = lax.dynamic_update_slice_in_dim(grad_cat, block_dcat, first, 0)
        token_grad_rows = lax.dynamic_update_slice_in_dim(token_grad_rows, block_tgrad, first, 0)
        route_grad = lax.dynamic_update_slice_in_dim(route_grad, block_route, first, 0)
        return (hidden, grad_cat, token_grad_rows, route_grad)

    return lax.fori_loop(jnp.int32(0), jnp.asarray(live_count), block_step, initial)


def weight_sum(rows_x, grad_cat, live_count, offset, length):
    offset_index = jnp.asarray(offset).astype(jnp.int32)

    def add_block(block_index, running):
        first = (block_index * BLK).astype(jnp.int32)
        block_rows = lax.dynamic_slice(rows_x, (first, offset_index), (BLK, length))
        block_dcat = lax.dynamic_slice_in_dim(grad_cat, first, BLK, 0)
        return running + lax.dot_general(
            block_rows, block_dcat, (((0,), (0,)), ((), ())), preferred_element_type=jnp.float32
        )

    return lax.fori_loop(
        jnp.int32(0),
        jnp.asarray(live_count),
        add_block,
        jnp.zeros((length, grad_cat.shape[1]), jnp.float32),
    )


def shards(tokens, route_w, w_gate, w_up, slot_token, slot_pick, live_blocks, d_hidden):
    tok_all = slot_token[0, 0]
    pick_all = slot_pick[0, 0]
    live_count = live_blocks[0, 0]
    cot_all = d_hidden[0, 0]
    hidden_width = w_gate.shape[2]
    rows_x = tokens[tok_all]
    gate_col = route_w[tok_all, pick_all]
    w_cat = jnp.concatenate((w_gate[0], w_up[0]), axis=1)
    w_full = lax.all_gather(w_cat, "dp", axis=0, tiled=True)
    hidden, grad_cat, token_grad_rows, route_grad = run_blocks(
        rows_x, gate_col, cot_all, w_full, live_count
    )
    token_grad = (
        jnp.zeros((tokens.shape[0], tokens.shape[1]), jnp.float32).at[tok_all].add(token_grad_rows)
    )
    route_part = jnp.zeros(route_w.shape, jnp.float32).at[tok_all, pick_all].add(route_grad)
    token_sum, route_sum = (
        lax.psum_scatter(
            token_grad.astype(jnp.bfloat16), "own", scatter_dimension=0, tiled=True
        ).astype(jnp.float32),
        lax.psum_scatter(
            route_part.astype(jnp.bfloat16), "own", scatter_dimension=0, tiled=True
        ).astype(jnp.float32),
    )
    summed = lax.psum_scatter(
        weight_sum(rows_x, grad_cat, live_count, 0, tokens.shape[1]).astype(jnp.bfloat16),
        "dp",
        scatter_dimension=0,
        tiled=True,
    ).astype(jnp.float32)
    grad_scale = 1.0 / math.sqrt(tokens.shape[0] * lax.axis_size("dp"))
    summed = summed * grad_scale
    return (
        hidden[None, None],
        summed[:, :hidden_width][None],
        summed[:, hidden_width:][None],
        token_sum.astype(jnp.bfloat16),
        route_sum,
    )


def ring_pos(index, n):
    return jnp.where(lax.rem(index, 2) == 0, index // 2, n - 1 - index // 2)


def ring_index(pos, n):
    return jnp.where(pos < n // 2, 2 * pos, 2 * (n - 1 - pos) + 1)


def tile_of(size, wanted):
    tile = wanted
    while size % tile:
        tile -= 128
    return tile


def moe_kernel(
    n, n_own, scale,
    live_ref, tok_col, tok_row, pick_col, route_t, tokens_hbm, wg_hbm, wu_hbm, cot_hbm,
    hidden_ref, gg_ref, gu_ref, dtok_ref, droute_ref,
    tokens_v, cot_v, wg_v, wu_v, x3, onehot, gcol, acc_g, acc_u, dcat_g, dcat_u,
    rows_v, slab_out, slab_in, red_g, red_u,
    local_sem, ag_send, ag_recv, rs_send, rs_recv, own_send, own_recv,
):
    cap = tok_col.shape[0]
    n_tok, width = tokens_v.shape
    hw = wg_v.shape[1]
    depth = width // n
    half = depth // 2
    cols = hw // 2
    part = n_tok // n_own
    wide = rows_v.shape[1]
    me = lax.axis_index("dp")
    own = lax.axis_index("own")
    pos = ring_pos(me, n)
    right = ring_index(lax.rem(pos + 1, n), n)
    left = ring_index(lax.rem(pos + n - 1, n), n)

    def owner_of(shift):
        return ring_index(lax.rem(pos + n + shift, n), n)

    def row_start(owner, piece):
        return pl.multiple_of(owner * depth + piece * half, half)

    locals_ = (
        pltpu.make_async_copy(tokens_hbm, tokens_v, local_sem.at[0]),
        pltpu.make_async_copy(cot_hbm, cot_v, local_sem.at[1]),
        pltpu.make_async_copy(wg_hbm, wg_v.at[pl.ds(row_start(me, 0), depth)], local_sem.at[2]),
        pltpu.make_async_copy(wu_hbm, wu_v.at[pl.ds(row_start(me, 0), depth)], local_sem.at[3]),
    )
    for copy in locals_:
        copy.start()

    barrier = pltpu.get_barrier_semaphore()
    for neighbour in (left, right):
        pl.semaphore_signal(
            barrier, inc=1, device_id=(neighbour, own), device_id_type=pl.DeviceIdType.MESH
        )
    for offset in range(1, n_own):
        pl.semaphore_signal(
            barrier, inc=1, device_id=(me, lax.rem(own + offset, n_own)),
            device_id_type=pl.DeviceIdType.MESH,
        )
    pl.semaphore_wait(barrier, 1 + n_own)

    def gather_copy(way, piece, step, first=False):
        buf, peer = (wg_v, right) if way == 0 else (wu_v, left)
        owner = owner_of(-step if way == 0 else step)
        dst = buf.at[pl.ds(row_start(owner, piece), half)]
        src = dst
        if first:
            src = (wg_hbm, wu_hbm)[way].at[pl.ds(piece * half, half)]
        return pltpu.make_async_remote_copy(
            src_ref=src, dst_ref=dst,
            send_sem=ag_send.at[way, piece, step], recv_sem=ag_recv.at[way, piece, step],
            device_id=(peer, own), device_id_type=pl.DeviceIdType.MESH,
        )

    for piece in range(2):
        for way in range(2):
            gather_copy(way, piece, 0, True).start()

    tile = 128
    slots = cap // tile

    locals_[0].wait()

    @pl.loop(0, slots)
    def _(t):
        r = pl.ds(pl.multiple_of(t * tile, tile), tile)
        hit = tok_col[r, :] == lax.broadcasted_iota(jnp.int32, (tile, n_tok), 1)
        onehot[r, :] = jnp.where(hit, 1.0, 0.0).astype(BF16)
        chosen = jnp.where(pick_col[r, :] == 0, route_t[0:1, :], route_t[1:2, :])
        g = jnp.sum(jnp.where(hit, chosen, 0.0), axis=1, keepdims=True)
        gcol[r, :] = jnp.broadcast_to(g, (tile, 128))

    @pl.loop(0, n // 2)
    def _(t):
        c = pl.ds(pl.multiple_of(t * 2 * depth, 2 * depth), 2 * depth)
        both = jnp.dot(onehot[...], tokens_v[:, c], preferred_element_type=F32).astype(BF16)
        x3[2 * t] = both[:, :depth]
        x3[2 * t + 1] = both[:, depth:]

    for copy in locals_[2:]:
        copy.wait()
    mine = pl.ds(row_start(me, 0), depth)
    acc_g[...] = jnp.dot(x3[me], wg_v[mine, :], preferred_element_type=F32)
    acc_u[...] = jnp.dot(x3[me], wu_v[mine, :], preferred_element_type=F32)

    @pl.loop(0, n - 1)
    def _(step):
        for piece in range(2):
            for way in range(2):
                got = owner_of(-step - 1 if way == 0 else step + 1)
                buf = (wg_v, wu_v)[way]
                here = buf.at[pl.ds(row_start(got, piece), half)]
                pltpu.make_async_remote_copy(
                    src_ref=here, dst_ref=here,
                    send_sem=ag_send.at[way, piece, step], recv_sem=ag_recv.at[way, piece, step],
                    device_id=((left, right)[way], own), device_id_type=pl.DeviceIdType.MESH,
                ).wait_recv()

                @pl.when(step < n - 2)
                def _():
                    gather_copy(way, piece, step + 1).start()

        og = owner_of(-step - 1)
        ou = owner_of(step + 1)
        acc_g[...] += jnp.dot(
            x3[og], wg_v[pl.ds(row_start(og, 0), depth), :], preferred_element_type=F32
        )
        acc_u[...] += jnp.dot(
            x3[ou], wu_v[pl.ds(row_start(ou, 0), depth), :], preferred_element_type=F32
        )

    locals_[1].wait()
    live = live_ref[0, 0] * BLK
    ftile = 64

    @pl.loop(0, cap // ftile)
    def _(t):
        start = pl.multiple_of(t * ftile, ftile)
        r = pl.ds(start, ftile)
        a = acc_g[r, :]
        u = acc_u[r, :]
        g = gcol[r, 0:1]
        cot = cot_v[r, :].astype(F32)
        alive = (lax.broadcasted_iota(jnp.int32, (ftile, hw), 0) + start) < live
        sig = jax.nn.sigmoid(a)
        act = a * sig
        hidden_ref[r, :] = jnp.where(alive, act * u * g, 0.0).astype(BF16)
        z = cot * g
        pa = z * u * sig * (1.0 + a * (1.0 - sig))
        dcat_g[r, :] = jnp.where(alive, pa, 0.0).astype(BF16)
        dcat_u[r, :] = jnp.where(alive, z * act, 0.0).astype(BF16)
        q = jnp.sum(jnp.where(alive, cot * act * u, 0.0), axis=1, keepdims=True)
        lane = lax.broadcasted_iota(jnp.int32, (ftile, 128), 1)
        rows_v[r, width:] = jnp.where(lane == pick_col[r, :], q, 0.0).astype(BF16)

    def term(way, owner, piece):
        dcat = (dcat_g, dcat_u)[way]
        return lax.dot_general(
            x3[owner], dcat[:, piece * cols:(piece + 1) * cols], (((0,), (0,)), ((), ())),
            preferred_element_type=F32,
        )

    def reduce_copy(way, piece, step, src_slot):
        red, peer = (red_g, right) if way == 0 else (red_u, left)
        return pltpu.make_async_remote_copy(
            src_ref=red.at[src_slot, piece], dst_ref=red.at[step, piece],
            send_sem=rs_send.at[way, piece, step], recv_sem=rs_recv.at[way, piece, step],
            device_id=(peer, own), device_id_type=pl.DeviceIdType.MESH,
        )

    for piece in range(2):
        for way in range(2):
            red = (red_g, red_u)[way]
            owner = owner_of(-1 if way == 0 else 1)
            red[n - 1, piece] = term(way, owner, piece).astype(BF16)
            reduce_copy(way, piece, 0, n - 1).start()

    ctile = tile_of(width, 512)

    @pl.loop(0, width // ctile)
    def _(t):
        c = pl.ds(pl.multiple_of(t * ctile, ctile), ctile)
        dims = (((1,), (1,)), ((), ()))
        total = lax.dot_general(dcat_g[...], wg_v[c, :], dims, preferred_element_type=F32)
        total += lax.dot_general(dcat_u[...], wu_v[c, :], dims, preferred_element_type=F32)
        rows_v[:, c] = total.astype(BF16)

    stile = tile_of(wide, 384)

    def slab_copy(offset):
        return pltpu.make_async_remote_copy(
            src_ref=slab_out.at[offset], dst_ref=slab_in.at[offset - 1],
            send_sem=own_send.at[offset - 1], recv_sem=own_recv.at[offset - 1],
            device_id=(me, lax.rem(own + offset, n_own)), device_id_type=pl.DeviceIdType.MESH,
        )

    def make_slab(offset):
        first = lax.rem(own + offset, n_own) * part
        hit = (lax.broadcasted_iota(jnp.int32, (part, cap), 0) + first) == tok_row[...]
        spread = jnp.where(hit, 1.0, 0.0).astype(BF16)

        @pl.loop(0, wide // stile)
        def _(t):
            c = pl.ds(pl.multiple_of(t * stile, stile), stile)
            slab_out[offset, :, c] = jnp.dot(
                spread, rows_v[:, c], preferred_element_type=F32
            ).astype(BF16)

    for offset in range(1, n_own):
        make_slab(offset)
        slab_copy(offset).start()

    @pl.loop(1, n - 1)
    def _(step):
        for piece in range(2):
            for way in range(2):
                red = (red_g, red_u)[way]
                owner = owner_of(-1 - step if way == 0 else 1 + step)
                add = term(way, owner, piece)
                reduce_copy(way, piece, step - 1, step - 1).wait_recv()
                red[step - 1, piece] = (red[step - 1, piece].astype(F32) + add).astype(BF16)
                reduce_copy(way, piece, step, step - 1).start()

    make_slab(0)

    for piece in range(2):
        for way in range(2):
            red = (red_g, red_u)[way]
            out = (gg_ref, gu_ref)[way]
            add = term(way, me, piece)
            reduce_copy(way, piece, n - 2, n - 2).wait_recv()
            out[:, piece * cols:(piece + 1) * cols] = (
                red[n - 2, piece].astype(F32) + add
            ) * scale

    for offset in range(1, n_own):
        slab_copy(offset).wait_recv()

    def slab_sum(c):
        total = slab_out[0, :, c].astype(F32)
        for k in range(n_own - 1):
            total = total + slab_in[k, :, c].astype(F32)
        return total

    @pl.loop(0, width // ctile)
    def _(t):
        c = pl.ds(pl.multiple_of(t * ctile, ctile), ctile)
        dtok_ref[:, c] = slab_sum(c).astype(BF16)

    droute_ref[...] = slab_sum(pl.ds(width, 128))

    for offset in range(1, n_own):
        slab_copy(offset).wait_send()

    for piece in range(2):
        for way in range(2):
            gather_copy(way, piece, 0, True).wait_send()
            reduce_copy(way, piece, 0, n - 1).wait_send()

    @pl.loop(1, n - 1)
    def _(step):
        for piece in range(2):
            for way in range(2):
                gather_copy(way, piece, step).wait_send()
                reduce_copy(way, piece, step, step - 1).wait_send()


def fused(n, n_own, tokens, route_w, w_gate, w_up, slot_token, slot_pick, live_blocks, d_hidden):
    n_tok, width = tokens.shape
    depth, hw = w_gate.shape[1:]
    cap = slot_token.shape[2]
    part = n_tok // n_own
    scale = 1.0 / math.sqrt(n_tok * n)
    vmem = pl.BlockSpec(memory_space=pltpu.VMEM)
    hbm = pl.BlockSpec(memory_space=pl.ANY)
    flops = 6 * cap * width * 2 * hw
    outs = pl.pallas_call(
        functools.partial(moe_kernel, n, n_own, scale),
        out_shape=(
            jax.ShapeDtypeStruct((cap, hw), BF16),
            jax.ShapeDtypeStruct((depth, hw), F32),
            jax.ShapeDtypeStruct((depth, hw), F32),
            jax.ShapeDtypeStruct((part, width), BF16),
            jax.ShapeDtypeStruct((part, 128), F32),
        ),
        in_specs=[pl.BlockSpec(memory_space=pltpu.SMEM)] + [vmem] * 4 + [hbm] * 4,
        out_specs=[vmem] * 5,
        scratch_shapes=[
            pltpu.VMEM((n_tok, width), BF16),
            pltpu.VMEM((cap, hw), BF16),
            pltpu.VMEM((width, hw), BF16),
            pltpu.VMEM((width, hw), BF16),
            pltpu.VMEM((n, cap, depth), BF16),
            pltpu.VMEM((cap, n_tok), BF16),
            pltpu.VMEM((cap, 128), F32),
            pltpu.VMEM((cap, hw), F32),
            pltpu.VMEM((cap, hw), F32),
            pltpu.VMEM((cap, hw), BF16),
            pltpu.VMEM((cap, hw), BF16),
            pltpu.VMEM((cap, width + 128), BF16),
            pltpu.VMEM((n_own, part, width + 128), BF16),
            pltpu.VMEM((n_own - 1, part, width + 128), BF16),
            pltpu.VMEM((n, 2, depth, hw // 2), BF16),
            pltpu.VMEM((n, 2, depth, hw // 2), BF16),
            pltpu.SemaphoreType.DMA((4,)),
            pltpu.SemaphoreType.DMA((2, 2, n - 1)),
            pltpu.SemaphoreType.DMA((2, 2, n - 1)),
            pltpu.SemaphoreType.DMA((2, 2, n - 1)),
            pltpu.SemaphoreType.DMA((2, 2, n - 1)),
            pltpu.SemaphoreType.DMA((n_own - 1,)),
            pltpu.SemaphoreType.DMA((n_own - 1,)),
        ],
        compiler_params=pltpu.CompilerParams(
            collective_id=0, has_side_effects=True, vmem_limit_bytes=60 * 1024 * 1024
        ),
        cost_estimate=pl.CostEstimate(
            flops=flops, bytes_accessed=16 * 1024 * 1024, transcendentals=cap * hw
        ),
    )(
        live_blocks, slot_token.reshape(cap, 1), slot_token.reshape(1, cap),
        slot_pick.reshape(cap, 1), route_w.T, tokens, w_gate[0], w_up[0], d_hidden[0, 0],
    )
    hidden, grad_gate, grad_up, d_tokens, d_route = outs
    return (
        hidden[None, None], grad_gate[None], grad_up[None], d_tokens,
        d_route[:, : route_w.shape[1]],
    )


def local_part(n, n_own, *args):
    depth, hw = args[2].shape[1:]
    cap = args[4].shape[2]
    fits = (
        n % 2 == 0 and n > 3 and n_own > 1 and depth % 64 == 0 and hw % 256 == 0
        and cap % 128 == 0 and args[0].shape[0] % (128 * n_own) == 0 and args[1].shape[1] == 2
    )
    if fits:
        return fused(n, n_own, *args)
    return shards(*args)


def solution(mesh):
    in_specs = (
        P("dp", None),
        P("dp", None),
        P("own", "dp", None),
        P("own", "dp", None),
        P("dp", "own", None),
        P("dp", "own", None),
        P("dp", "own"),
        P("dp", "own", None, None),
    )
    out_specs = (
        P("dp", "own", None, None),
        P("own", "dp", None),
        P("own", "dp", None),
        P(("dp", "own"), None),
        P(("dp", "own"), None),
    )
    body = functools.partial(local_part, mesh.shape["dp"], mesh.shape["own"])
    return jax.shard_map(body, mesh=mesh, in_specs=in_specs, out_specs=out_specs, check_vma=False)
```

```python
import math
import functools

import jax
import jax.numpy as jnp
from jax import lax
from jax.experimental import pallas as pl
from jax.experimental.pallas import tpu as pltpu
from jax.sharding import PartitionSpec as P

BLK = 128
F32 = jnp.float32
BF16 = jnp.bfloat16


def finish(pre_gate, pre_up, block_gate, block_cot):
    sigmoid_gate = jax.nn.sigmoid(pre_gate)
    activated = pre_gate * sigmoid_gate
    block_hidden = (activated * pre_up * block_gate).astype(jnp.bfloat16)
    scaled_cot = block_cot * block_gate
    grad_pre = scaled_cot * pre_up * sigmoid_gate * (1.0 + pre_gate * (1.0 - sigmoid_gate))
    grad_up_pre = scaled_cot * activated
    grad_cat = jnp.concatenate(
        (grad_pre.astype(jnp.bfloat16), grad_up_pre.astype(jnp.bfloat16)), axis=1
    )
    route_grad = jnp.sum(block_cot * activated * pre_up, axis=1)
    return (block_hidden, grad_cat, route_grad)


def run_blocks(rows_x, gate_col, cot_all, w_full, live_count):
    capacity = rows_x.shape[0]
    hidden_width = w_full.shape[1] // 2
    initial = (
        jnp.zeros((capacity, hidden_width), jnp.bfloat16),
        jnp.zeros((capacity, 2 * hidden_width), jnp.bfloat16),
        jnp.zeros((capacity, w_full.shape[0]), jnp.float32),
        jnp.zeros((capacity,), jnp.float32),
    )

    def block_step(block_index, state_now):
        hidden, grad_cat, token_grad_rows, route_grad = state_now
        first = (block_index * BLK).astype(jnp.int32)
        block_rows = lax.dynamic_slice_in_dim(rows_x, first, BLK, 0)
        block_gate = lax.dynamic_slice_in_dim(gate_col, first, BLK, 0)[:, None]
        block_cot = lax.dynamic_slice_in_dim(cot_all, first, BLK, 0).astype(jnp.float32)
        projected = jnp.dot(block_rows, w_full, preferred_element_type=jnp.float32)
        block_hidden, block_dcat, block_route = finish(
            projected[:, :hidden_width], projected[:, hidden_width:], block_gate, block_cot
        )
        block_tgrad = lax.dot_general(
            block_dcat, w_full, (((1,), (1,)), ((), ())), preferred_element_type=jnp.float32
        )
        hidden = lax.dynamic_update_slice_in_dim(hidden, block_hidden, first, 0)
        grad_cat = lax.dynamic_update_slice_in_dim(grad_cat, block_dcat, first, 0)
        token_grad_rows = lax.dynamic_update_slice_in_dim(token_grad_rows, block_tgrad, first, 0)
        route_grad = lax.dynamic_update_slice_in_dim(route_grad, block_route, first, 0)
        return (hidden, grad_cat, token_grad_rows, route_grad)

    return lax.fori_loop(jnp.int32(0), jnp.asarray(live_count), block_step, initial)


def weight_sum(rows_x, grad_cat, live_count, offset, length):
    offset_index = jnp.asarray(offset).astype(jnp.int32)

    def add_block(block_index, running):
        first = (block_index * BLK).astype(jnp.int32)
        block_rows = lax.dynamic_slice(rows_x, (first, offset_index), (BLK, length))
        block_dcat = lax.dynamic_slice_in_dim(grad_cat, first, BLK, 0)
        return running + lax.dot_general(
            block_rows, block_dcat, (((0,), (0,)), ((), ())), preferred_element_type=jnp.float32
        )

    return lax.fori_loop(
        jnp.int32(0),
        jnp.asarray(live_count),
        add_block,
        jnp.zeros((length, grad_cat.shape[1]), jnp.float32),
    )


def shards(tokens, route_w, w_gate, w_up, slot_token, slot_pick, live_blocks, d_hidden):
    tok_all = slot_token[0, 0]
    pick_all = slot_pick[0, 0]
    live_count = live_blocks[0, 0]
    cot_all = d_hidden[0, 0]
    hidden_width = w_gate.shape[2]
    rows_x = tokens[tok_all]
    gate_col = route_w[tok_all, pick_all]
    w_cat = jnp.concatenate((w_gate[0], w_up[0]), axis=1)
    w_full = lax.all_gather(w_cat, "dp", axis=0, tiled=True)
    hidden, grad_cat, token_grad_rows, route_grad = run_blocks(
        rows_x, gate_col, cot_all, w_full, live_count
    )
    token_grad = (
        jnp.zeros((tokens.shape[0], tokens.shape[1]), jnp.float32).at[tok_all].add(token_grad_rows)
    )
    route_part = jnp.zeros(route_w.shape, jnp.float32).at[tok_all, pick_all].add(route_grad)
    token_sum, route_sum = (
        lax.psum_scatter(
            token_grad.astype(jnp.bfloat16), "own", scatter_dimension=0, tiled=True
        ).astype(jnp.float32),
        lax.psum_scatter(
            route_part.astype(jnp.bfloat16), "own", scatter_dimension=0, tiled=True
        ).astype(jnp.float32),
    )
    summed = lax.psum_scatter(
        weight_sum(rows_x, grad_cat, live_count, 0, tokens.shape[1]).astype(jnp.bfloat16),
        "dp",
        scatter_dimension=0,
        tiled=True,
    ).astype(jnp.float32)
    grad_scale = 1.0 / math.sqrt(tokens.shape[0] * lax.axis_size("dp"))
    summed = summed * grad_scale
    return (
        hidden[None, None],
        summed[:, :hidden_width][None],
        summed[:, hidden_width:][None],
        token_sum.astype(jnp.bfloat16),
        route_sum,
    )


def ring_pos(index, n):
    return jnp.where(lax.rem(index, 2) == 0, index // 2, n - 1 - index // 2)


def ring_index(pos, n):
    return jnp.where(pos < n // 2, 2 * pos, 2 * (n - 1 - pos) + 1)


def tile_of(size, wanted):
    tile = wanted
    while size % tile:
        tile -= 128
    return tile


def moe_kernel(
    n, n_own, scale,
    live_ref, tok_row, pick_row, route_t, tokens_hbm, wg_hbm, wu_hbm, cot_hbm,
    hidden_hbm, gg_ref, gu_ref, dtok_hbm, droute_ref,
    hidden_ref, dtok_ref, pick_col, qsum,
    tokens_v, cot_v, wg_v, wu_v, x3, onehot, gcol, acc_g, acc_u, dcat_g, dcat_u,
    rows_v, slab_out, slab_in, red_g, red_u,
    local_sem, ag_send, ag_recv, rs_send, rs_recv, own_send, own_recv,
):
    cap = tok_row.shape[1]
    n_tok, width = tokens_v.shape
    hw = wg_v.shape[1]
    depth = width // n
    cols = hw // 2
    part = n_tok // n_own
    wide = rows_v.shape[1]
    me = lax.axis_index("dp")
    own = lax.axis_index("own")
    pos = ring_pos(me, n)
    right = ring_index(lax.rem(pos + 1, n), n)
    left = ring_index(lax.rem(pos + n - 1, n), n)

    def owner_of(shift):
        return ring_index(lax.rem(pos + n + shift, n), n)

    def rows_of(owner):
        return pl.ds(pl.multiple_of(owner * depth, depth), depth)

    def cols_of(piece):
        return pl.ds(piece * cols, cols)

    locals_ = (
        pltpu.make_async_copy(tokens_hbm, tokens_v, local_sem.at[0]),
        pltpu.make_async_copy(cot_hbm, cot_v, local_sem.at[1]),
        pltpu.make_async_copy(wg_hbm, wg_v.at[rows_of(me)], local_sem.at[2]),
        pltpu.make_async_copy(wu_hbm, wu_v.at[rows_of(me)], local_sem.at[3]),
    )
    for copy in locals_:
        copy.start()

    barrier = pltpu.get_barrier_semaphore()
    for neighbour in (left, right):
        pl.semaphore_signal(
            barrier, inc=1, device_id=(neighbour, own), device_id_type=pl.DeviceIdType.MESH
        )
    for offset in range(1, n_own):
        pl.semaphore_signal(
            barrier, inc=1, device_id=(me, lax.rem(own + offset, n_own)),
            device_id_type=pl.DeviceIdType.MESH,
        )
    pl.semaphore_wait(barrier, 1 + n_own)

    def gather_copy(way, piece, step, first=False):
        buf, peer = (wg_v, right) if way == 0 else (wu_v, left)
        owner = owner_of(-step if way == 0 else step)
        dst = buf.at[rows_of(owner), cols_of(piece)]
        src = dst
        if first:
            src = (wg_hbm, wu_hbm)[way].at[:, cols_of(piece)]
        return pltpu.make_async_remote_copy(
            src_ref=src, dst_ref=dst,
            send_sem=ag_send.at[way, piece, step], recv_sem=ag_recv.at[way, piece, step],
            device_id=(peer, own), device_id_type=pl.DeviceIdType.MESH,
        )

    for way in range(2):
        gather_copy(way, 0, 0, True).start()

    tile = 128
    locals_[0].wait()

    @pl.loop(0, cap // tile)
    def _(t):
        r = pl.ds(pl.multiple_of(t * tile, tile), tile)
        token = jnp.broadcast_to(tok_row[:, r], (tile, tile)).T
        pick = jnp.broadcast_to(pick_row[:, r], (tile, tile)).T
        pick_col[r, :] = pick
        hit = token[:, 0:1] == lax.broadcasted_iota(jnp.int32, (tile, n_tok), 1)
        onehot[r, :] = jnp.where(hit, 1.0, 0.0).astype(BF16)
        chosen = jnp.where(pick[:, 0:1] == 0, route_t[0:1, :], route_t[1:2, :])
        g = jnp.sum(jnp.where(hit, chosen, 0.0), axis=1, keepdims=True)
        gcol[r, :] = jnp.broadcast_to(g, (tile, 128))

    def owners_at(step):
        return owner_of(-step - 1), owner_of(step + 1)

    def take(piece, step):
        for way in range(2):
            here = (wg_v, wu_v)[way].at[rows_of(owners_at(step)[way]), cols_of(piece)]
            pltpu.make_async_remote_copy(
                src_ref=here, dst_ref=here,
                send_sem=ag_send.at[way, piece, step], recv_sem=ag_recv.at[way, piece, step],
                device_id=((left, right)[way], own), device_id_type=pl.DeviceIdType.MESH,
            ).wait_recv()

            @pl.when(step < n - 2)
            def _():
                gather_copy(way, piece, step + 1).start()

    def accumulate(piece, step):
        for way in range(2):
            owner = owners_at(step)[way]
            acc = (acc_g, acc_u)[way]
            acc[:, cols_of(piece)] += jnp.dot(
                x3[owner], (wg_v, wu_v)[way][rows_of(owner), cols_of(piece)],
                preferred_element_type=F32,
            )

    lag = 2
    take(0, 0)

    @pl.loop(0, n // 2)
    def _(t):
        c = pl.ds(pl.multiple_of(t * 2 * depth, 2 * depth), 2 * depth)
        both = jnp.dot(onehot[...], tokens_v[:, c], preferred_element_type=F32).astype(BF16)
        x3[2 * t] = both[:, :depth]
        x3[2 * t + 1] = both[:, depth:]

    take(0, 1)
    for way in range(2):
        gather_copy(way, 1, 0, True).start()
    for copy in locals_[2:]:
        copy.wait()
    acc_g[...] = jnp.dot(x3[me], wg_v[rows_of(me), :], preferred_element_type=F32)
    acc_u[...] = jnp.dot(x3[me], wu_v[rows_of(me), :], preferred_element_type=F32)
    for step in range(lag):
        accumulate(0, step)

    @pl.loop(lag, n - 1)
    def _(step):
        take(0, step)
        take(1, step - lag)
        accumulate(0, step)
        accumulate(1, step - lag)

    locals_[1].wait()
    live = live_ref[0, 0] * BLK
    ftile = 64

    def finish_piece(piece):
        @pl.loop(0, cap // ftile)
        def _(t):
            start = pl.multiple_of(t * ftile, ftile)
            r = pl.ds(start, ftile)
            c = cols_of(piece)
            a = acc_g[r, c]
            u = acc_u[r, c]
            g = gcol[r, 0:1]
            cot = cot_v[r, c].astype(F32)
            alive = (lax.broadcasted_iota(jnp.int32, (ftile, cols), 0) + start) < live
            sig = jax.nn.sigmoid(a)
            act = a * sig
            hidden_ref[r, c] = jnp.where(alive, act * u * g, 0.0).astype(BF16)
            z = cot * g
            pa = z * u * sig * (1.0 + a * (1.0 - sig))
            dcat_g[r, c] = jnp.where(alive, pa, 0.0).astype(BF16)
            dcat_u[r, c] = jnp.where(alive, z * act, 0.0).astype(BF16)
            q = jnp.sum(jnp.where(alive, cot * act * u, 0.0), axis=1, keepdims=True)
            if piece == 0:
                qsum[r, :] = jnp.broadcast_to(q, (ftile, 128))
            else:
                lane = lax.broadcasted_iota(jnp.int32, (ftile, 128), 1)
                rows_v[r, width:] = jnp.where(
                    lane == pick_col[r, :], qsum[r, :] + q, 0.0
                ).astype(BF16)

    def term(way, owner, piece):
        dcat = (dcat_g, dcat_u)[way]
        return lax.dot_general(
            x3[owner], dcat[:, piece * cols:(piece + 1) * cols], (((0,), (0,)), ((), ())),
            preferred_element_type=F32,
        )

    def reduce_copy(way, piece, step, src_slot):
        red, peer = (red_g, right) if way == 0 else (red_u, left)
        return pltpu.make_async_remote_copy(
            src_ref=red.at[src_slot, piece], dst_ref=red.at[step, piece],
            send_sem=rs_send.at[way, piece, step], recv_sem=rs_recv.at[way, piece, step],
            device_id=(peer, own), device_id_type=pl.DeviceIdType.MESH,
        )

    def reduce_first(piece):
        for way in range(2):
            red = (red_g, red_u)[way]
            owner = owner_of(-1 if way == 0 else 1)
            red[n - 1, piece] = term(way, owner, piece).astype(BF16)
            reduce_copy(way, piece, 0, n - 1).start()

    finish_piece(0)
    reduce_first(0)

    @pl.loop(n - 1 - lag, n - 1)
    def _(step):
        take(1, step)
        accumulate(1, step)

    finish_piece(1)
    reduce_first(1)
    hidden_out = pltpu.make_async_copy(hidden_ref, hidden_hbm, local_sem.at[4])
    hidden_out.start()

    ctile = tile_of(width, 512)

    @pl.loop(0, width // ctile)
    def _(t):
        c = pl.ds(pl.multiple_of(t * ctile, ctile), ctile)
        dims = (((1,), (1,)), ((), ()))
        total = lax.dot_general(dcat_g[...], wg_v[c, :], dims, preferred_element_type=F32)
        total += lax.dot_general(dcat_u[...], wu_v[c, :], dims, preferred_element_type=F32)
        rows_v[:, c] = total.astype(BF16)

    stile = tile_of(wide, 384)

    def slab_copy(offset):
        return pltpu.make_async_remote_copy(
            src_ref=slab_out.at[offset], dst_ref=slab_in.at[offset - 1],
            send_sem=own_send.at[offset - 1], recv_sem=own_recv.at[offset - 1],
            device_id=(me, lax.rem(own + offset, n_own)), device_id_type=pl.DeviceIdType.MESH,
        )

    def make_slab(offset):
        first = lax.rem(own + offset, n_own) * part
        hit = (lax.broadcasted_iota(jnp.int32, (part, cap), 0) + first) == tok_row[...]
        spread = jnp.where(hit, 1.0, 0.0).astype(BF16)

        @pl.loop(0, wide // stile)
        def _(t):
            c = pl.ds(pl.multiple_of(t * stile, stile), stile)
            slab_out[offset, :, c] = jnp.dot(
                spread, rows_v[:, c], preferred_element_type=F32
            ).astype(BF16)

    def reduce_step(step):
        for piece in range(2):
            for way in range(2):
                red = (red_g, red_u)[way]
                owner = owner_of(-1 - step if way == 0 else 1 + step)
                add = term(way, owner, piece)
                reduce_copy(way, piece, step - 1, step - 1).wait_recv()
                red[step - 1, piece] = (red[step - 1, piece].astype(F32) + add).astype(BF16)
                reduce_copy(way, piece, step, step - 1).start()

    mixed = min(n - 2, n_own - 1)
    for offset in range(1, mixed + 1):
        reduce_step(offset)
        make_slab(offset)
        slab_copy(offset).start()
    for offset in range(mixed + 1, n_own):
        make_slab(offset)
        slab_copy(offset).start()

    @pl.loop(mixed + 1, n - 1)
    def _(step):
        reduce_step(step)

    make_slab(0)

    for offset in range(1, n_own):
        slab_copy(offset).wait_recv()

    def slab_sum(c):
        total = slab_out[0, :, c].astype(F32)
        for k in range(n_own - 1):
            total = total + slab_in[k, :, c].astype(F32)
        return total

    @pl.loop(0, width // ctile)
    def _(t):
        c = pl.ds(pl.multiple_of(t * ctile, ctile), ctile)
        dtok_ref[:, c] = slab_sum(c).astype(BF16)

    droute_ref[...] = slab_sum(pl.ds(width, 128)).T[0:droute_ref.shape[0], :]
    dtok_out = pltpu.make_async_copy(dtok_ref, dtok_hbm, local_sem.at[5])
    dtok_out.start()

    for piece in range(2):
        for way in range(2):
            red = (red_g, red_u)[way]
            out = (gg_ref, gu_ref)[way]
            add = term(way, me, piece)
            reduce_copy(way, piece, n - 2, n - 2).wait_recv()
            out[:, piece * cols:(piece + 1) * cols] = (
                red[n - 2, piece].astype(F32) + add
            ) * scale

    hidden_out.wait()
    dtok_out.wait()
    for offset in range(1, n_own):
        slab_copy(offset).wait_send()

    for piece in range(2):
        for way in range(2):
            gather_copy(way, piece, 0, True).wait_send()
            reduce_copy(way, piece, 0, n - 1).wait_send()

    @pl.loop(1, n - 1)
    def _(step):
        for piece in range(2):
            for way in range(2):
                gather_copy(way, piece, step).wait_send()
                reduce_copy(way, piece, step, step - 1).wait_send()


def place_kernel(*refs):
    copies = [pltpu.make_async_copy(refs[k], refs[5 + k], refs[10].at[k]) for k in range(5)]
    for copy in copies:
        copy.start()
    for copy in copies:
        copy.wait()


def fused(n, n_own, tokens, route_w, w_gate, w_up, slot_token, slot_pick, live_blocks, d_hidden):
    n_tok, width = tokens.shape
    depth, hw = w_gate.shape[1:]
    cap = slot_token.shape[2]
    part = n_tok // n_own
    scale = 1.0 / math.sqrt(n_tok * n)
    vmem = pl.BlockSpec(memory_space=pltpu.VMEM)
    hbm = pl.BlockSpec(memory_space=pl.ANY)
    flops = 6 * cap * width * 2 * hw
    outs = pl.pallas_call(
        functools.partial(moe_kernel, n, n_own, scale),
        out_shape=(
            jax.ShapeDtypeStruct((cap, hw), BF16),
            jax.ShapeDtypeStruct((depth, hw), F32),
            jax.ShapeDtypeStruct((depth, hw), F32),
            jax.ShapeDtypeStruct((part, width), BF16),
            jax.ShapeDtypeStruct((route_w.shape[1], part), F32),
        ),
        in_specs=[pl.BlockSpec(memory_space=pltpu.SMEM)] + [vmem] * 3 + [hbm] * 4,
        out_specs=[hbm, vmem, vmem, hbm, vmem],
        scratch_shapes=[
            pltpu.VMEM((cap, hw), BF16),
            pltpu.VMEM((part, width), BF16),
            pltpu.VMEM((cap, 128), jnp.int32),
            pltpu.VMEM((cap, 128), F32),
            pltpu.VMEM((n_tok, width), BF16),
            pltpu.VMEM((cap, hw), BF16),
            pltpu.VMEM((width, hw), BF16),
            pltpu.VMEM((width, hw), BF16),
            pltpu.VMEM((n, cap, depth), BF16),
            pltpu.VMEM((cap, n_tok), BF16),
            pltpu.VMEM((cap, 128), F32),
            pltpu.VMEM((cap, hw), F32),
            pltpu.VMEM((cap, hw), F32),
            pltpu.VMEM((cap, hw), BF16),
            pltpu.VMEM((cap, hw), BF16),
            pltpu.VMEM((cap, width + 128), BF16),
            pltpu.VMEM((n_own, part, width + 128), BF16),
            pltpu.VMEM((n_own - 1, part, width + 128), BF16),
            pltpu.VMEM((n, 2, depth, hw // 2), BF16),
            pltpu.VMEM((n, 2, depth, hw // 2), BF16),
            pltpu.SemaphoreType.DMA((6,)),
            pltpu.SemaphoreType.DMA((2, 2, n - 1)),
            pltpu.SemaphoreType.DMA((2, 2, n - 1)),
            pltpu.SemaphoreType.DMA((2, 2, n - 1)),
            pltpu.SemaphoreType.DMA((2, 2, n - 1)),
            pltpu.SemaphoreType.DMA((n_own - 1,)),
            pltpu.SemaphoreType.DMA((n_own - 1,)),
        ],
        compiler_params=pltpu.CompilerParams(
            collective_id=0, has_side_effects=True, vmem_limit_bytes=60 * 1024 * 1024
        ),
        cost_estimate=pl.CostEstimate(
            flops=flops, bytes_accessed=16 * 1024 * 1024, transcendentals=cap * hw
        ),
    )(
        live_blocks, slot_token.reshape(1, cap), slot_pick.reshape(1, cap), route_w.T, tokens, w_gate[0], w_up[0], d_hidden[0, 0],
    )
    hidden, grad_gate, grad_up, d_tokens, d_route = pl.pallas_call(
        place_kernel,
        out_shape=tuple(jax.ShapeDtypeStruct(o.shape, o.dtype) for o in outs),
        in_specs=[hbm] * 5,
        out_specs=[hbm] * 5,
        scratch_shapes=[pltpu.SemaphoreType.DMA((5,))],
        cost_estimate=pl.CostEstimate(
            flops=0, bytes_accessed=8 * 1024 * 1024, transcendentals=0
        ),
    )(*outs)
    return (
        hidden[None, None], grad_gate[None], grad_up[None], d_tokens,
        d_route.T,
    )


def local_part(n, n_own, *args):
    depth, hw = args[2].shape[1:]
    cap = args[4].shape[2]
    fits = (
        n % 2 == 0 and n > 3 and n_own > 1 and depth % 64 == 0 and hw % 256 == 0
        and cap % 128 == 0 and args[0].shape[0] % (128 * n_own) == 0 and args[1].shape[1] == 2
    )
    if fits:
        return fused(n, n_own, *args)
    return shards(*args)


def solution(mesh):
    in_specs = (
        P("dp", None),
        P("dp", None),
        P("own", "dp", None),
        P("own", "dp", None),
        P("dp", "own", None),
        P("dp", "own", None),
        P("dp", "own"),
        P("dp", "own", None, None),
    )
    out_specs = (
        P("dp", "own", None, None),
        P("own", "dp", None),
        P("own", "dp", None),
        P(("dp", "own"), None),
        P(("dp", "own"), None),
    )
    body = functools.partial(local_part, mesh.shape["dp"], mesh.shape["own"])
    return jax.shard_map(body, mesh=mesh, in_specs=in_specs, out_specs=out_specs, check_vma=False)
```

```python
import math
import functools

import jax
import jax.numpy as jnp
from jax import lax
from jax.experimental import pallas as pl
from jax.experimental.pallas import tpu as pltpu
from jax.sharding import PartitionSpec as P

BLK = 128
F32 = jnp.float32
BF16 = jnp.bfloat16


def finish(pre_gate, pre_up, block_gate, block_cot):
    sigmoid_gate = jax.nn.sigmoid(pre_gate)
    activated = pre_gate * sigmoid_gate
    block_hidden = (activated * pre_up * block_gate).astype(jnp.bfloat16)
    scaled_cot = block_cot * block_gate
    grad_pre = scaled_cot * pre_up * sigmoid_gate * (1.0 + pre_gate * (1.0 - sigmoid_gate))
    grad_up_pre = scaled_cot * activated
    grad_cat = jnp.concatenate(
        (grad_pre.astype(jnp.bfloat16), grad_up_pre.astype(jnp.bfloat16)), axis=1
    )
    route_grad = jnp.sum(block_cot * activated * pre_up, axis=1)
    return (block_hidden, grad_cat, route_grad)


def run_blocks(rows_x, gate_col, cot_all, w_full, live_count):
    capacity = rows_x.shape[0]
    hidden_width = w_full.shape[1] // 2
    initial = (
        jnp.zeros((capacity, hidden_width), jnp.bfloat16),
        jnp.zeros((capacity, 2 * hidden_width), jnp.bfloat16),
        jnp.zeros((capacity, w_full.shape[0]), jnp.float32),
        jnp.zeros((capacity,), jnp.float32),
    )

    def block_step(block_index, state_now):
        hidden, grad_cat, token_grad_rows, route_grad = state_now
        first = (block_index * BLK).astype(jnp.int32)
        block_rows = lax.dynamic_slice_in_dim(rows_x, first, BLK, 0)
        block_gate = lax.dynamic_slice_in_dim(gate_col, first, BLK, 0)[:, None]
        block_cot = lax.dynamic_slice_in_dim(cot_all, first, BLK, 0).astype(jnp.float32)
        projected = jnp.dot(block_rows, w_full, preferred_element_type=jnp.float32)
        block_hidden, block_dcat, block_route = finish(
            projected[:, :hidden_width], projected[:, hidden_width:], block_gate, block_cot
        )
        block_tgrad = lax.dot_general(
            block_dcat, w_full, (((1,), (1,)), ((), ())), preferred_element_type=jnp.float32
        )
        hidden = lax.dynamic_update_slice_in_dim(hidden, block_hidden, first, 0)
        grad_cat = lax.dynamic_update_slice_in_dim(grad_cat, block_dcat, first, 0)
        token_grad_rows = lax.dynamic_update_slice_in_dim(token_grad_rows, block_tgrad, first, 0)
        route_grad = lax.dynamic_update_slice_in_dim(route_grad, block_route, first, 0)
        return (hidden, grad_cat, token_grad_rows, route_grad)

    return lax.fori_loop(jnp.int32(0), jnp.asarray(live_count), block_step, initial)


def weight_sum(rows_x, grad_cat, live_count, offset, length):
    offset_index = jnp.asarray(offset).astype(jnp.int32)

    def add_block(block_index, running):
        first = (block_index * BLK).astype(jnp.int32)
        block_rows = lax.dynamic_slice(rows_x, (first, offset_index), (BLK, length))
        block_dcat = lax.dynamic_slice_in_dim(grad_cat, first, BLK, 0)
        return running + lax.dot_general(
            block_rows, block_dcat, (((0,), (0,)), ((), ())), preferred_element_type=jnp.float32
        )

    return lax.fori_loop(
        jnp.int32(0),
        jnp.asarray(live_count),
        add_block,
        jnp.zeros((length, grad_cat.shape[1]), jnp.float32),
    )


def shards(tokens, route_w, w_gate, w_up, slot_token, slot_pick, live_blocks, d_hidden):
    tok_all = slot_token[0, 0]
    pick_all = slot_pick[0, 0]
    live_count = live_blocks[0, 0]
    cot_all = d_hidden[0, 0]
    hidden_width = w_gate.shape[2]
    rows_x = tokens[tok_all]
    gate_col = route_w[tok_all, pick_all]
    w_cat = jnp.concatenate((w_gate[0], w_up[0]), axis=1)
    w_full = lax.all_gather(w_cat, "dp", axis=0, tiled=True)
    hidden, grad_cat, token_grad_rows, route_grad = run_blocks(
        rows_x, gate_col, cot_all, w_full, live_count
    )
    token_grad = (
        jnp.zeros((tokens.shape[0], tokens.shape[1]), jnp.float32).at[tok_all].add(token_grad_rows)
    )
    route_part = jnp.zeros(route_w.shape, jnp.float32).at[tok_all, pick_all].add(route_grad)
    token_sum, route_sum = (
        lax.psum_scatter(
            token_grad.astype(jnp.bfloat16), "own", scatter_dimension=0, tiled=True
        ).astype(jnp.float32),
        lax.psum_scatter(
            route_part.astype(jnp.bfloat16), "own", scatter_dimension=0, tiled=True
        ).astype(jnp.float32),
    )
    summed = lax.psum_scatter(
        weight_sum(rows_x, grad_cat, live_count, 0, tokens.shape[1]).astype(jnp.bfloat16),
        "dp",
        scatter_dimension=0,
        tiled=True,
    ).astype(jnp.float32)
    grad_scale = 1.0 / math.sqrt(tokens.shape[0] * lax.axis_size("dp"))
    summed = summed * grad_scale
    return (
        hidden[None, None],
        summed[:, :hidden_width][None],
        summed[:, hidden_width:][None],
        token_sum.astype(jnp.bfloat16),
        route_sum,
    )


def ring_pos(index, n):
    return jnp.where(lax.rem(index, 2) == 0, index // 2, n - 1 - index // 2)


def ring_index(pos, n):
    return jnp.where(pos < n // 2, 2 * pos, 2 * (n - 1 - pos) + 1)


def tile_of(size, wanted):
    tile = wanted
    while size % tile:
        tile -= 128
    return tile


def moe_kernel(
    n, n_own, scale,
    live_ref, tok_row, pick_row, route_t, tokens_hbm, wg_hbm, wu_hbm, cot_hbm,
    hidden_hbm, gg_ref, gu_ref, dtok_hbm, droute_ref,
    hidden_ref, dtok_ref, pick_col, qsum,
    tokens_v, cot_v, wg_v, wu_v, x3, onehot, gcol, acc_g, acc_u, dcat_g, dcat_u,
    rows_v, slab_out, slab_in, red_g, red_u,
    local_sem, ag_send, ag_recv, rs_send, rs_recv, own_send, own_recv,
):
    cap = tok_row.shape[1]
    n_tok, width = tokens_v.shape
    hw = wg_v.shape[1]
    depth = width // n
    cols = hw // 2
    part = n_tok // n_own
    wide = rows_v.shape[1]
    me = lax.axis_index("dp")
    own = lax.axis_index("own")
    pos = ring_pos(me, n)
    right = ring_index(lax.rem(pos + 1, n), n)
    left = ring_index(lax.rem(pos + n - 1, n), n)

    def owner_of(shift):
        return ring_index(lax.rem(pos + n + shift, n), n)

    def rows_of(owner):
        return pl.ds(pl.multiple_of(owner * depth, depth), depth)

    def cols_of(piece):
        return pl.ds(piece * cols, cols)

    locals_ = (
        pltpu.make_async_copy(tokens_hbm, tokens_v, local_sem.at[0]),
        pltpu.make_async_copy(cot_hbm, cot_v, local_sem.at[1]),
        pltpu.make_async_copy(wg_hbm, wg_v.at[rows_of(me)], local_sem.at[2]),
        pltpu.make_async_copy(wu_hbm, wu_v.at[rows_of(me)], local_sem.at[3]),
    )
    for copy in locals_:
        copy.start()

    barrier = pltpu.get_barrier_semaphore()
    for neighbour in (left, right):
        pl.semaphore_signal(
            barrier, inc=1, device_id=(neighbour, own), device_id_type=pl.DeviceIdType.MESH
        )
    for offset in range(1, n_own):
        pl.semaphore_signal(
            barrier, inc=1, device_id=(me, lax.rem(own + offset, n_own)),
            device_id_type=pl.DeviceIdType.MESH,
        )
    pl.semaphore_wait(barrier, 1 + n_own)

    def gather_copy(way, piece, step, first=False):
        buf, peer = (wg_v, right) if way == 0 else (wu_v, left)
        owner = owner_of(-step if way == 0 else step)
        dst = buf.at[rows_of(owner), cols_of(piece)]
        src = dst
        if first:
            src = (wg_hbm, wu_hbm)[way].at[:, cols_of(piece)]
        return pltpu.make_async_remote_copy(
            src_ref=src, dst_ref=dst,
            send_sem=ag_send.at[way, piece, step], recv_sem=ag_recv.at[way, piece, step],
            device_id=(peer, own), device_id_type=pl.DeviceIdType.MESH,
        )

    for way in range(2):
        gather_copy(way, 0, 0, True).start()

    tile = 128
    locals_[0].wait()

    @pl.loop(0, cap // tile)
    def _(t):
        r = pl.ds(pl.multiple_of(t * tile, tile), tile)
        token = jnp.broadcast_to(tok_row[:, r], (tile, tile)).T
        pick = jnp.broadcast_to(pick_row[:, r], (tile, tile)).T
        pick_col[r, :] = pick
        hit = token[:, 0:1] == lax.broadcasted_iota(jnp.int32, (tile, n_tok), 1)
        onehot[r, :] = jnp.where(hit, 1.0, 0.0).astype(BF16)
        chosen = jnp.where(pick[:, 0:1] == 0, route_t[0:1, :], route_t[1:2, :])
        g = jnp.sum(jnp.where(hit, chosen, 0.0), axis=1, keepdims=True)
        gcol[r, :] = jnp.broadcast_to(g, (tile, 128))

    def owners_at(step):
        return owner_of(-step - 1), owner_of(step + 1)

    def take(piece, step):
        for way in range(2):
            here = (wg_v, wu_v)[way].at[rows_of(owners_at(step)[way]), cols_of(piece)]
            pltpu.make_async_remote_copy(
                src_ref=here, dst_ref=here,
                send_sem=ag_send.at[way, piece, step], recv_sem=ag_recv.at[way, piece, step],
                device_id=((left, right)[way], own), device_id_type=pl.DeviceIdType.MESH,
            ).wait_recv()

            @pl.when(step < n - 2)
            def _():
                gather_copy(way, piece, step + 1).start()

    def accumulate(piece, step):
        for way in range(2):
            owner = owners_at(step)[way]
            acc = (acc_g, acc_u)[way]
            acc[:, cols_of(piece)] += jnp.dot(
                x3[owner], (wg_v, wu_v)[way][rows_of(owner), cols_of(piece)],
                preferred_element_type=F32,
            )

    lag = 2
    take(0, 0)

    @pl.loop(0, n // 2)
    def _(t):
        c = pl.ds(pl.multiple_of(t * 2 * depth, 2 * depth), 2 * depth)
        both = jnp.dot(onehot[...], tokens_v[:, c], preferred_element_type=F32).astype(BF16)
        x3[2 * t] = both[:, :depth]
        x3[2 * t + 1] = both[:, depth:]

    take(0, 1)
    for way in range(2):
        gather_copy(way, 1, 0, True).start()
    for copy in locals_[2:]:
        copy.wait()
    acc_g[...] = jnp.dot(x3[me], wg_v[rows_of(me), :], preferred_element_type=F32)
    acc_u[...] = jnp.dot(x3[me], wu_v[rows_of(me), :], preferred_element_type=F32)
    for step in range(lag):
        accumulate(0, step)

    @pl.loop(lag, n - 1)
    def _(step):
        take(0, step)
        take(1, step - lag)
        accumulate(0, step)
        accumulate(1, step - lag)

    locals_[1].wait()
    live = live_ref[0, 0] * BLK
    ftile = 64

    def finish_piece(piece):
        @pl.loop(0, cap // ftile)
        def _(t):
            start = pl.multiple_of(t * ftile, ftile)
            r = pl.ds(start, ftile)
            c = cols_of(piece)
            a = acc_g[r, c]
            u = acc_u[r, c]
            g = gcol[r, 0:1]
            cot = cot_v[r, c].astype(F32)
            alive = (lax.broadcasted_iota(jnp.int32, (ftile, cols), 0) + start) < live
            sig = jax.nn.sigmoid(a)
            act = a * sig
            hidden_ref[r, c] = jnp.where(alive, act * u * g, 0.0).astype(BF16)
            z = cot * g
            pa = z * u * sig * (1.0 + a * (1.0 - sig))
            dcat_g[r, c] = jnp.where(alive, pa, 0.0).astype(BF16)
            dcat_u[r, c] = jnp.where(alive, z * act, 0.0).astype(BF16)
            q = jnp.sum(jnp.where(alive, cot * act * u, 0.0), axis=1, keepdims=True)
            if piece == 0:
                qsum[r, :] = jnp.broadcast_to(q, (ftile, 128))
            else:
                lane = lax.broadcasted_iota(jnp.int32, (ftile, 128), 1)
                rows_v[r, width:] = jnp.where(
                    lane == pick_col[r, :], qsum[r, :] + q, 0.0
                ).astype(BF16)

    def term(way, owner, piece):
        dcat = (dcat_g, dcat_u)[way]
        return lax.dot_general(
            x3[owner], dcat[:, piece * cols:(piece + 1) * cols], (((0,), (0,)), ((), ())),
            preferred_element_type=F32,
        )

    def reduce_copy(way, piece, step, src_slot):
        red, peer = (red_g, right) if way == 0 else (red_u, left)
        return pltpu.make_async_remote_copy(
            src_ref=red.at[src_slot, piece], dst_ref=red.at[step, piece],
            send_sem=rs_send.at[way, piece, step], recv_sem=rs_recv.at[way, piece, step],
            device_id=(peer, own), device_id_type=pl.DeviceIdType.MESH,
        )

    def reduce_first(piece):
        for way in range(2):
            red = (red_g, red_u)[way]
            owner = owner_of(-1 if way == 0 else 1)
            red[n - 1, piece] = term(way, owner, piece).astype(BF16)
            reduce_copy(way, piece, 0, n - 1).start()

    finish_piece(0)
    reduce_first(0)

    @pl.loop(n - 1 - lag, n - 1)
    def _(step):
        take(1, step)
        accumulate(1, step)

    finish_piece(1)
    reduce_first(1)
    hidden_out = pltpu.make_async_copy(hidden_ref, hidden_hbm, local_sem.at[4])
    hidden_out.start()

    ctile = tile_of(width, 512)

    @pl.loop(0, width // ctile)
    def _(t):
        c = pl.ds(pl.multiple_of(t * ctile, ctile), ctile)
        dims = (((1,), (1,)), ((), ()))
        total = lax.dot_general(dcat_g[...], wg_v[c, :], dims, preferred_element_type=F32)
        total += lax.dot_general(dcat_u[...], wu_v[c, :], dims, preferred_element_type=F32)
        rows_v[:, c] = total.astype(BF16)

    stile = tile_of(wide, 384)

    def slab_copy(offset):
        return pltpu.make_async_remote_copy(
            src_ref=slab_out.at[offset], dst_ref=slab_in.at[offset - 1],
            send_sem=own_send.at[offset - 1], recv_sem=own_recv.at[offset - 1],
            device_id=(me, lax.rem(own + offset, n_own)), device_id_type=pl.DeviceIdType.MESH,
        )

    def make_slab(offset):
        first = lax.rem(own + offset, n_own) * part
        hit = (lax.broadcasted_iota(jnp.int32, (part, cap), 0) + first) == tok_row[...]
        spread = jnp.where(hit, 1.0, 0.0).astype(BF16)

        @pl.loop(0, wide // stile)
        def _(t):
            c = pl.ds(pl.multiple_of(t * stile, stile), stile)
            slab_out[offset, :, c] = jnp.dot(
                spread, rows_v[:, c], preferred_element_type=F32
            ).astype(BF16)

    def reduce_step(step):
        for piece in range(2):
            for way in range(2):
                red = (red_g, red_u)[way]
                owner = owner_of(-1 - step if way == 0 else 1 + step)
                add = term(way, owner, piece)
                reduce_copy(way, piece, step - 1, step - 1).wait_recv()
                red[step - 1, piece] = (red[step - 1, piece].astype(F32) + add).astype(BF16)
                reduce_copy(way, piece, step, step - 1).start()

    mixed = min(n - 2, n_own - 1)
    for offset in range(1, mixed + 1):
        reduce_step(offset)
        make_slab(offset)
        slab_copy(offset).start()
    for offset in range(mixed + 1, n_own):
        make_slab(offset)
        slab_copy(offset).start()

    @pl.loop(mixed + 1, n - 1)
    def _(step):
        reduce_step(step)

    make_slab(0)

    for offset in range(1, n_own):
        slab_copy(offset).wait_recv()

    def slab_sum(c):
        total = slab_out[0, :, c].astype(F32)
        for k in range(n_own - 1):
            total = total + slab_in[k, :, c].astype(F32)
        return total

    @pl.loop(0, width // ctile)
    def _(t):
        c = pl.ds(pl.multiple_of(t * ctile, ctile), ctile)
        dtok_ref[:, c] = slab_sum(c).astype(BF16)

    droute_ref[...] = slab_sum(pl.ds(width, 128)).T[0:droute_ref.shape[0], :]
    dtok_out = pltpu.make_async_copy(dtok_ref, dtok_hbm, local_sem.at[5])
    dtok_out.start()

    for piece in range(2):
        for way in range(2):
            red = (red_g, red_u)[way]
            out = (gg_ref, gu_ref)[way]
            add = term(way, me, piece)
            reduce_copy(way, piece, n - 2, n - 2).wait_recv()
            out[:, piece * cols:(piece + 1) * cols] = (
                red[n - 2, piece].astype(F32) + add
            ) * scale

    hidden_out.wait()
    dtok_out.wait()
    for offset in range(1, n_own):
        slab_copy(offset).wait_send()

    for piece in range(2):
        for way in range(2):
            gather_copy(way, piece, 0, True).wait_send()
            reduce_copy(way, piece, 0, n - 1).wait_send()

    @pl.loop(1, n - 1)
    def _(step):
        for piece in range(2):
            for way in range(2):
                gather_copy(way, piece, step).wait_send()
                reduce_copy(way, piece, step, step - 1).wait_send()


def place_kernel(*refs):
    sems = refs[15]
    into = [pltpu.make_async_copy(refs[k], refs[10 + k], sems.at[0, k]) for k in range(5)]
    out = [pltpu.make_async_copy(refs[10 + k], refs[5 + k], sems.at[1, k]) for k in range(5)]
    for copy in into:
        copy.start()
    for k in range(5):
        into[k].wait()
        out[k].start()
    for copy in out:
        copy.wait()


def fused(n, n_own, tokens, route_w, w_gate, w_up, slot_token, slot_pick, live_blocks, d_hidden):
    n_tok, width = tokens.shape
    depth, hw = w_gate.shape[1:]
    cap = slot_token.shape[2]
    part = n_tok // n_own
    scale = 1.0 / math.sqrt(n_tok * n)
    vmem = pl.BlockSpec(memory_space=pltpu.VMEM)
    hbm = pl.BlockSpec(memory_space=pl.ANY)
    flops = 6 * cap * width * 2 * hw
    outs = pl.pallas_call(
        functools.partial(moe_kernel, n, n_own, scale),
        out_shape=(
            jax.ShapeDtypeStruct((cap, hw), BF16),
            jax.ShapeDtypeStruct((depth, hw), F32),
            jax.ShapeDtypeStruct((depth, hw), F32),
            jax.ShapeDtypeStruct((part, width), BF16),
            jax.ShapeDtypeStruct((route_w.shape[1], part), F32),
        ),
        in_specs=[pl.BlockSpec(memory_space=pltpu.SMEM)] + [vmem] * 3 + [hbm] * 4,
        out_specs=[hbm, vmem, vmem, hbm, vmem],
        scratch_shapes=[
            pltpu.VMEM((cap, hw), BF16),
            pltpu.VMEM((part, width), BF16),
            pltpu.VMEM((cap, 128), jnp.int32),
            pltpu.VMEM((cap, 128), F32),
            pltpu.VMEM((n_tok, width), BF16),
            pltpu.VMEM((cap, hw), BF16),
            pltpu.VMEM((width, hw), BF16),
            pltpu.VMEM((width, hw), BF16),
            pltpu.VMEM((n, cap, depth), BF16),
            pltpu.VMEM((cap, n_tok), BF16),
            pltpu.VMEM((cap, 128), F32),
            pltpu.VMEM((cap, hw), F32),
            pltpu.VMEM((cap, hw), F32),
            pltpu.VMEM((cap, hw), BF16),
            pltpu.VMEM((cap, hw), BF16),
            pltpu.VMEM((cap, width + 128), BF16),
            pltpu.VMEM((n_own, part, width + 128), BF16),
            pltpu.VMEM((n_own - 1, part, width + 128), BF16),
            pltpu.VMEM((n, 2, depth, hw // 2), BF16),
            pltpu.VMEM((n, 2, depth, hw // 2), BF16),
            pltpu.SemaphoreType.DMA((6,)),
            pltpu.SemaphoreType.DMA((2, 2, n - 1)),
            pltpu.SemaphoreType.DMA((2, 2, n - 1)),
            pltpu.SemaphoreType.DMA((2, 2, n - 1)),
            pltpu.SemaphoreType.DMA((2, 2, n - 1)),
            pltpu.SemaphoreType.DMA((n_own - 1,)),
            pltpu.SemaphoreType.DMA((n_own - 1,)),
        ],
        compiler_params=pltpu.CompilerParams(
            collective_id=0, has_side_effects=True, vmem_limit_bytes=60 * 1024 * 1024
        ),
        cost_estimate=pl.CostEstimate(
            flops=flops, bytes_accessed=16 * 1024 * 1024, transcendentals=cap * hw
        ),
    )(
        live_blocks, slot_token.reshape(1, cap), slot_pick.reshape(1, cap), route_w.T, tokens, w_gate[0], w_up[0], d_hidden[0, 0],
    )
    hidden, grad_gate, grad_up, d_tokens, d_route = pl.pallas_call(
        place_kernel,
        out_shape=tuple(jax.ShapeDtypeStruct(o.shape, o.dtype) for o in outs),
        in_specs=[hbm] * 5,
        out_specs=[hbm] * 5,
        scratch_shapes=[pltpu.VMEM(o.shape, o.dtype) for o in outs]
        + [pltpu.SemaphoreType.DMA((2, 5))],
        compiler_params=pltpu.CompilerParams(vmem_limit_bytes=32 * 1024 * 1024),
        cost_estimate=pl.CostEstimate(
            flops=0, bytes_accessed=8 * 1024 * 1024, transcendentals=0
        ),
    )(*outs)
    return (
        hidden[None, None], grad_gate[None], grad_up[None], d_tokens,
        d_route.T,
    )


def local_part(n, n_own, *args):
    depth, hw = args[2].shape[1:]
    cap = args[4].shape[2]
    fits = (
        n % 2 == 0 and n > 3 and n_own > 1 and depth % 64 == 0 and hw % 256 == 0
        and cap % 128 == 0 and args[0].shape[0] % (128 * n_own) == 0 and args[1].shape[1] == 2
    )
    if fits:
        return fused(n, n_own, *args)
    return shards(*args)


def solution(mesh):
    in_specs = (
        P("dp", None),
        P("dp", None),
        P("own", "dp", None),
        P("own", "dp", None),
        P("dp", "own", None),
        P("dp", "own", None),
        P("dp", "own"),
        P("dp", "own", None, None),
    )
    out_specs = (
        P("dp", "own", None, None),
        P("own", "dp", None),
        P("own", "dp", None),
        P(("dp", "own"), None),
        P(("dp", "own"), None),
    )
    body = functools.partial(local_part, mesh.shape["dp"], mesh.shape["own"])
    return jax.shard_map(body, mesh=mesh, in_specs=in_specs, out_specs=out_specs, check_vma=False)
```
